32 devices in a mesh: row: 4 (over y, x), col: 8 (over z, core).
Axes of the slice: x: 2, y: 2, z: 4, core: 2. Of those that a mesh axis runs over, the one named last changes fastest.
Arguments:
- inputs: bfloat16 [1024, 8192], P('col', 'row'), may hold values from -6 to 6
- upstream: bfloat16 [1024, 8192], P('col', 'row'), may hold values from -6 to 6
- w_gate: bfloat16 [8192, 14784], P('row', 'col'), may hold values from -0.0625 to 0.0625
- w_up: bfloat16 [8192, 14784], P('row', 'col'), may hold values from -0.0625 to 0.0625
- w_down: bfloat16 [14784, 8192], P('col', 'row'), may hold values from -0.046875 to 0.046875
Outputs:
- grad_in: bfloat16 [1024, 8192], P('col', 'row')
- grad_gate: bfloat16 [8192, 14784], P('row', 'col')
- grad_up: bfloat16 [8192, 14784], P('row', 'col')
- grad_down: bfloat16 [14784, 8192], P('col', 'row')
The draws below stay inside these ranges and needn't reach their ends.
All inputs are finite; a program needn't handle non-finite values.
Results may differ from the reference program's by a relative error of at most 0.02.
Values may be sent and summed in bfloat16 or wider, within the bound.
No kernel may reach another device: no remote copies, remote signals or barrier semaphores. Data moves between devices by JAX's collectives and lax.ppermute only.
A program may use at most 192 MiB of HBM per device.

```python
import jax
import jax.numpy as jnp
from jax import lax

D = 8192
FF = 14784
TOKENS = 1024
DBLK = 2048
FBLK = 1848


def levels(rng, shape, split, least, top_value):
    factor_of = 1.0
    for dim, parts in split:
        draws = jax.random.uniform(jax.random.fold_in(jax.random.fold_in(rng, 6), dim), (parts,), jnp.float32, least / len(split), top_value / len(split))
        factor_of = factor_of * jnp.repeat(jnp.exp(draws), shape[dim] // parts).reshape((-1,) + (1,) * (len(shape) - 1 - dim))
    return factor_of


def gaussian(rng, extent, spread, limit, split=(), kind=jnp.bfloat16):
    drawn = jax.random.normal(rng, extent, jnp.float32) * spread
    if len(split) > 0:
        drawn = levels(rng, extent, split, -0.22, 0.18) * drawn
    return jnp.clip(drawn, min=-limit, max=limit).astype(kind)


def setup_inputs(seed: int = 0) -> dict:
    seeds = jax.random.split(jax.random.key(seed), 6)
    inputs = gaussian(seeds[0], (TOKENS, D), 1.0, 6.0, ((0, 8), (1, 4)))
    upstream = gaussian(seeds[1], (TOKENS, D), 1.0, 6.0, ((0, 8), (1, 4)))
    w_gate = gaussian(seeds[2], (D, FF), D ** -0.5, 0.0625, ((0, 4), (1, 8)))
    w_up = gaussian(seeds[3], (D, FF), D ** -0.5, 0.0625, ((0, 4), (1, 8)))
    w_down = gaussian(seeds[4], (FF, D), FF ** -0.5, 0.046875, ((0, 8), (1, 4)))
    return dict(inputs=inputs, upstream=upstream, w_gate=w_gate, w_up=w_up, w_down=w_down)


def blockwise(left, right_t):
    total = jnp.zeros((left.shape[0], right_t.shape[0]), jnp.float32)

    def step(carry, index):
        start = (index * DBLK).astype(jnp.int32)
        piece = lax.dynamic_slice_in_dim(left, start, DBLK, 1)
        weight = lax.dynamic_slice_in_dim(right_t, start, DBLK, 1)
        term = lax.dot_general(piece, weight, (((1,), (1,)), ((), ())), preferred_element_type=jnp.float32)
        rounded = lax.optimization_barrier(term.astype(jnp.bfloat16))
        return carry + rounded.astype(jnp.float32), None

    total, unused = lax.scan(step, total, jnp.arange(D // DBLK, dtype=jnp.int32))
    return total


def input_blocks(d_gate, d_up, w_gate, w_up):
    total = jnp.zeros((d_gate.shape[0], w_gate.shape[0]), jnp.float32)
    back = (((1,), (1,)), ((), ()))

    def step(carry, index):
        start = (index * FBLK).astype(jnp.int32)
        gate_part = lax.dynamic_slice_in_dim(d_gate, start, FBLK, 1)
        up_part = lax.dynamic_slice_in_dim(d_up, start, FBLK, 1)
        gate_w = lax.dynamic_slice_in_dim(w_gate, start, FBLK, 1)
        up_w = lax.dynamic_slice_in_dim(w_up, start, FBLK, 1)
        term = lax.dot_general(gate_part, gate_w, back, preferred_element_type=jnp.float32)
        term = term + lax.dot_general(up_part, up_w, back, preferred_element_type=jnp.float32)
        rounded = lax.optimization_barrier(term.astype(jnp.bfloat16))
        return carry + rounded.astype(jnp.float32), None

    total, unused = lax.scan(step, total, jnp.arange(FF // FBLK, dtype=jnp.int32))
    return total


def reference(inputs, upstream, w_gate, w_up, w_down):
    gate = blockwise(inputs, w_gate.T)
    up = blockwise(inputs, w_up.T)
    d_hidden = blockwise(upstream, w_down)
    sig = 1.0 / (1.0 + jnp.exp(-gate))
    silu = gate * sig
    hidden = (silu * up).astype(jnp.bfloat16)
    d_up = (d_hidden * silu).astype(jnp.bfloat16)
    d_gate = (d_hidden * up * sig * (1.0 + gate * (1.0 - sig))).astype(jnp.bfloat16)
    contract = (((0,), (0,)), ((), ()))
    grad_down = lax.dot_general(hidden, upstream, contract, preferred_element_type=jnp.float32).astype(jnp.bfloat16)
    grad_gate = lax.dot_general(inputs, d_gate, contract, preferred_element_type=jnp.float32).astype(jnp.bfloat16)
    grad_up = lax.dot_general(inputs, d_up, contract, preferred_element_type=jnp.float32).astype(jnp.bfloat16)
    grad_in = input_blocks(d_gate, d_up, w_gate, w_up)
    return grad_in.astype(jnp.bfloat16), grad_gate, grad_up, grad_down
```

```python
import functools

import jax
import jax.numpy as jnp
from jax import lax
from jax.experimental import pallas as pl
from jax.experimental.pallas import tpu as pltpu
from jax.sharding import PartitionSpec as P

BF = jnp.bfloat16
F32 = jnp.float32
VMEM_LIMIT = 56 * 1024 * 1024
TINY = pl.CostEstimate(flops=1, bytes_accessed=1, transcendentals=0)


def activations(gate, up, d_hidden):
    sig = 1.0 / (1.0 + jnp.exp(-gate))
    silu = gate * sig
    hidden = (silu * up).astype(BF)
    d_up = (d_hidden * silu).astype(BF)
    d_gate = (d_hidden * up * sig * (1.0 + gate * (1.0 - sig))).astype(BF)
    return hidden, d_gate, d_up


def general(inputs, upstream, w_gate, w_up, w_down):
    x_all = lax.all_gather(inputs, "col", axis=0, tiled=True)
    dy_all = lax.all_gather(upstream, "col", axis=0, tiled=True)
    back = (((1,), (1,)), ((), ()))
    terms = (
        jnp.dot(x_all, w_gate, preferred_element_type=F32),
        jnp.dot(x_all, w_up, preferred_element_type=F32),
        lax.dot_general(dy_all, w_down, back, preferred_element_type=F32),
    )
    sums = [
        lax.psum_scatter(t.astype(BF), "row", scatter_dimension=0, tiled=True).astype(F32)
        for t in terms
    ]
    hidden, d_gate, d_up = (
        lax.all_gather(a, "row", axis=0, tiled=True) for a in activations(*sums)
    )
    contract = (((0,), (0,)), ((), ()))
    grad_down = lax.dot_general(hidden, dy_all, contract, preferred_element_type=F32).astype(BF)
    grad_gate = lax.dot_general(x_all, d_gate, contract, preferred_element_type=F32).astype(BF)
    grad_up = lax.dot_general(x_all, d_up, contract, preferred_element_type=F32).astype(BF)
    term = lax.dot_general(d_gate, w_gate, back, preferred_element_type=F32)
    term = term + lax.dot_general(d_up, w_up, back, preferred_element_type=F32)
    grad_in = lax.psum_scatter(term.astype(BF), "col", scatter_dimension=0, tiled=True)
    return grad_in, grad_gate, grad_up, grad_down


def quarter_rows(width):
    return -(-width // 64) * 16


def masked(block, quarter, width):
    rows = block.shape[0]
    index = quarter * rows + lax.broadcasted_iota(jnp.int32, block.shape, 0)
    return jnp.where(index < width, block, jnp.zeros_like(block))


def order_only():
    return pl.BlockSpec(memory_space=pl.ANY)


def gate(a, after):
    return pl.pallas_call(
        lambda *refs: None,
        out_shape=jax.ShapeDtypeStruct(a.shape, a.dtype),
        in_specs=[order_only()] * (1 + len(after)),
        out_specs=order_only(),
        input_output_aliases={0: 0},
        cost_estimate=TINY,
    )(a, *after)


def entry_spec(a, index):
    if index is None:
        return pl.BlockSpec(a.shape, lambda s, p: (0,) * a.ndim)
    return pl.BlockSpec((None,) + a.shape[1:], lambda s, p: (index,) + (0,) * (a.ndim - 1))


SEND_FIRST = ((1, 0), (1, 1), (0, 0), (0, 1))
ORDER = ((0, 0), (0, 1), (1, 0), (1, 1))


def terms_kernel(width, n, lefts, place, *refs):
    kinds = sorted(set(lefts))
    blocks = refs[: n * len(kinds)]
    weights = refs[n * len(kinds) : n * len(kinds) + len(lefts)]
    send_a, keep_a, send_b, keep_b, both = refs[-5:]
    step = pl.program_id(0)
    tok = blocks[0].shape[0]

    @pl.when(step == 0)
    def _():
        for i, r in enumerate(blocks):
            both[i // n, (i % n) * tok : (i % n + 1) * tok, :] = r[...]

    dims = (((1,), (1,)), ((), ()))
    cut = n * tok // 2
    for i, w in enumerate(weights):
        left = both[kinds.index(lefts[i])]
        t = lax.dot_general(w[...], left, dims, preferred_element_type=F32)
        t = masked(t, place[step], width).astype(BF)
        for s, (dx, dy) in enumerate(SEND_FIRST):

            @pl.when(step == s)
            def _(t=t, i=i, dx=dx, dy=dy):
                (send_a if dx else keep_a)[dy, i] = t[:, :cut]
                (send_b if dy else keep_b)[dx, i] = t[:, cut:]


def terms(place, blocks, weights, lefts, after):
    n = len(blocks)
    used = [b[k] for k in sorted(set(lefts)) for b in blocks]
    width, feats = weights[0].shape
    rows = quarter_rows(width)
    tok = used[0][0].shape[-2]
    weight = pl.BlockSpec((rows, feats), lambda s, p: (p[s], 0))
    shape = (2, len(weights), rows, n * tok // 2)
    part = pl.BlockSpec(shape, lambda s, p: (0, 0, 0, 0))
    return pl.pallas_call(
        functools.partial(terms_kernel, width, n, lefts),
        out_shape=[jax.ShapeDtypeStruct(shape, BF)] * 4,
        grid_spec=pltpu.PrefetchScalarGridSpec(
            num_scalar_prefetch=1,
            grid=(4,),
            in_specs=[entry_spec(*e) for e in used]
            + [weight] * len(weights)
            + [order_only()] * len(after),
            out_specs=[part] * 4,
            scratch_shapes=[pltpu.VMEM((len(set(lefts)), n * tok, feats), BF)],
        ),
        compiler_params=pltpu.CompilerParams(vmem_limit_bytes=VMEM_LIMIT),
        cost_estimate=TINY,
    )(place, *[a for a, _ in used], *weights, *after)


def halves_kernel(groups, *refs):
    per = 2 * len(groups)
    for side in range(2):
        mine, out = refs[side * per : (side + 1) * per], refs[len(refs) - 2 + side]
        for g, group in enumerate(groups):
            for k, i in enumerate(group):
                total = mine[2 * g][0, k].astype(F32) + mine[2 * g + 1][0, k].astype(F32)
                out[i] = total.astype(BF)


def halves(groups, got, after):
    rows, tok = got[0][0].shape[2:]
    arrays = [v for ka, ra, _, _ in got for v in (ka, ra)]
    arrays += [v for _, _, kb, rb in got for v in (kb, rb)]
    specs = [pl.BlockSpec((1,) + a.shape[1:], lambda s: (1, 0, 0, 0)) for a in arrays]
    out = jax.ShapeDtypeStruct((3, rows, tok), BF)
    return pl.pallas_call(
        functools.partial(halves_kernel, groups),
        out_shape=[out, out],
        grid=(1,),
        in_specs=specs + [order_only()] * len(after),
        out_specs=[pl.BlockSpec(out.shape, lambda s: (0, 0, 0))] * 2,
        compiler_params=pltpu.CompilerParams(vmem_limit_bytes=VMEM_LIMIT),
        cost_estimate=TINY,
    )(*arrays, *after)


def act_kernel(groups, earlier, per, *refs):
    outs = refs[-4:]
    for side in range(2):
        mine = refs[side * per : (side + 1) * per]
        last = mine[2 * len(groups)]
        sums = [None] * 3
        for g, group in enumerate(groups):
            for k, i in enumerate(group):
                keep, got = mine[2 * g], mine[2 * g + 1]
                sums[i] = keep[0, k].astype(F32) + got[0, k].astype(F32) + last[i].astype(F32)
        hidden, d_gate, d_up = activations(*sums)
        d, h = outs[2 * side], outs[2 * side + 1]
        tok = hidden.shape[1]
        d[0, :, -tok:], d[1, :, -tok:], h[:, -tok:] = d_gate, d_up, hidden
        if "d" in earlier:
            d[:, :, :-tok] = mine[2 * len(groups) + 1][...]
        if "h" in earlier:
            h[:, :-tok] = mine[-1][...]


def act(groups, sides, earlier, after):
    rows, tok = sides[0][0].shape[2:]
    specs = []
    for a in sides[0]:
        block = (1,) + a.shape[1:] if a.ndim == 4 else a.shape
        specs.append(pl.BlockSpec(block, lambda s, n=a.ndim: (0,) * n))
    before = {k: sides[0][-len(earlier) + i].shape[-1] for i, k in enumerate(earlier)}
    d = jax.ShapeDtypeStruct((2, rows, before.get("d", 0) + tok), BF)
    h = jax.ShapeDtypeStruct((rows, before.get("h", 0) + tok), BF)
    dspec = pl.BlockSpec(d.shape, lambda s: (0, 0, 0))
    hspec = pl.BlockSpec(h.shape, lambda s: (0, 0))
    return pl.pallas_call(
        functools.partial(act_kernel, groups, earlier, len(specs)),
        out_shape=[d, h, d, h],
        grid=(1,),
        in_specs=specs * 2 + [order_only()] * len(after),
        out_specs=[dspec, hspec, dspec, hspec],
        compiler_params=pltpu.CompilerParams(vmem_limit_bytes=VMEM_LIMIT),
        cost_estimate=TINY,
    )(*sides[0], *sides[1], *after)


def gin_kernel(width, n, place, *refs):
    quarters, (wg, wu) = refs[: 4 * n], refs[4 * n : 4 * n + 2]
    ta, tb, total = refs[-3:]
    step = pl.program_id(0)
    dims = (((0,), (0,)), ((), ()))
    wgm = masked(wg[...], place[step], width)
    wum = masked(wu[...], place[step], width)
    for s in range(4):

        @pl.when(step == s)
        def _(s=s):
            mine = quarters[s * n : (s + 1) * n]
            dg = jnp.concatenate([r[0] for r in mine], axis=1)
            du = jnp.concatenate([r[1] for r in mine], axis=1)
            t = lax.dot_general(dg, wgm, dims, preferred_element_type=F32)
            t = t + lax.dot_general(du, wum, dims, preferred_element_type=F32)
            if s == 0:
                total[...] = t
            elif s < 3:
                total[...] += t
            else:
                t = t + total[...]
                blocks, tok, _ = ta.shape
                for j in range(blocks):
                    ta[j] = t[j * tok : (j + 1) * tok].astype(BF)
                    tb[j] = t[(blocks + j) * tok : (blocks + j + 1) * tok].astype(BF)


def gin(place, quarters, wg, wu, tok, after):
    n = len(quarters[0])
    width, feats = wg.shape
    rows = quarters[0][0][0].shape[-2]
    blocks = sum(a.shape[-1] for a, _ in quarters[0]) // (2 * tok)
    specs = [entry_spec(*e) for q in quarters for e in q]
    weight = pl.BlockSpec((rows, feats), lambda s, p: (p[s], 0))
    out = pl.BlockSpec((blocks, tok, feats), lambda s, p: (0, 0, 0))
    return pl.pallas_call(
        functools.partial(gin_kernel, width, n),
        out_shape=[jax.ShapeDtypeStruct((blocks, tok, feats), BF)] * 2,
        grid_spec=pltpu.PrefetchScalarGridSpec(
            num_scalar_prefetch=1,
            grid=(4,),
            in_specs=specs + [weight, weight] + [order_only()] * len(after),
            out_specs=[out, out],
            scratch_shapes=[pltpu.VMEM((2 * blocks * tok, feats), F32)],
        ),
        compiler_params=pltpu.CompilerParams(vmem_limit_bytes=VMEM_LIMIT),
        cost_estimate=TINY,
    )(place, *[a for q in quarters for a, _ in q], wg, wu, *after)


def wgrad_kernel(kinds, n, blocks, place, *refs):
    left, right = refs[: 4 * n], refs[4 * n : 4 * n + blocks]
    outs, toks = refs[-1 - kinds : -1], refs[-1]
    step = pl.program_id(0)
    tok = right[0].shape[0]

    @pl.when(step == 0)
    def _():
        for b in range(blocks):
            toks[b * tok : (b + 1) * tok, :] = right[b][...]

    for s in range(4):

        @pl.when(step == s)
        def _(s=s):
            mine = left[s * n : (s + 1) * n]
            for k in range(kinds):
                m = jnp.concatenate([r[k] if kinds > 1 else r[...] for r in mine], axis=1)
                outs[k][...] = jnp.dot(m, toks[...], preferred_element_type=F32).astype(BF)


def wgrad(place, left, right, kinds, width, after):
    n, blocks = len(left[0]), len(right)
    rows = left[0][0][0].shape[-2]
    tok, feats = right[0][0].shape[-2:]
    lspecs = [entry_spec(*e) for q in left for e in q]
    rspecs = [entry_spec(*e) for e in right]
    out = pl.BlockSpec((rows, feats), lambda s, p: (p[s], 0))
    return pl.pallas_call(
        functools.partial(wgrad_kernel, kinds, n, blocks),
        out_shape=[jax.ShapeDtypeStruct((width, feats), BF)] * kinds,
        grid_spec=pltpu.PrefetchScalarGridSpec(
            num_scalar_prefetch=1,
            grid=(4,),
            in_specs=lspecs + rspecs + [order_only()] * len(after),
            out_specs=[out] * kinds,
            scratch_shapes=[pltpu.VMEM((blocks * tok, feats), BF)],
        ),
        compiler_params=pltpu.CompilerParams(vmem_limit_bytes=VMEM_LIMIT),
        cost_estimate=TINY,
    )(place, *[a for q in left for a, _ in q], *[a for a, _ in right], *after)


def grid_4_8(inputs, upstream, w_gate, w_up, w_down):
    weights = (w_gate.T, w_up.T, w_down)
    wg, wu, _ = weights
    width = w_down.shape[0]
    tok = inputs.shape[0]
    row = lax.axis_index("row").astype(jnp.int32)
    x, y = row % 2, row // 2

    def place_of(pairs):
        return jnp.stack([2 * (x ^ dx) + (y ^ dy) for dx, dy in pairs])

    place_t, place_g = place_of(SEND_FIRST), place_of(ORDER)

    def over_row(a, bit):
        return lax.ppermute(a, "row", [(r, r ^ bit) for r in range(4)])

    def over_col(a, bits):
        return lax.ppermute(a, "col", [(c, c ^ bits) for c in range(8)])

    px, py = functools.partial(over_row, bit=1), functools.partial(over_row, bit=2)

    own = jnp.stack([inputs, upstream])
    def swapped(pair):
        return tuple((over_col(a if i is None else a[i], 1), None) for a, i in pair)

    def halved(a):
        return ((a, 0), (a, 1))

    even = [((inputs, None), (upstream, None))]
    odd = [swapped(even[0])]
    z1, z2 = over_col(own, 2), over_col(own, 4)

    split, together = ((0, 1), (2,)), ((0, 1, 2),)

    def start_sums(blocks, group, after):
        sa, ka, sb, kb = terms(
            place_t,
            [e[j] for e in (even, odd) for j in blocks],
            [weights[i] for i in group],
            [i // 2 for i in group],
            after,
        )
        return ka, px(sa), kb, py(sb)

    def finish(groups, got, qa, qb, before, after):
        sides = [
            [v for ka, ra, _, _ in got for v in (ka, ra)] + [qa],
            [v for _, _, kb, rb in got for v in (kb, rb)] + [qb],
        ]
        earlier = "".join(k for k, _ in before)
        for _, pair in before:
            for side, a in zip(sides, pair):
                side.append(a)
        da, ha, db, hb = act(groups, sides, earlier, after)
        return (da, db), (ha, hb)

    def gather_first(a, b):
        return jnp.stack([a, py(a)]), jnp.stack([b, px(b)])

    def gather_second(sa, sb):
        return sa, sb, px(sa), py(sb)

    def quarters(sa, sb, ra, rb):
        return (
            ((sa, 0), (sb, 0)),
            ((sa, 1), (rb, 0)),
            ((ra, 0), (sb, 1)),
            ((ra, 1), (rb, 1)),
        )

    got0 = start_sums([0], together[0], [])
    even.append(halved(gate(z1, [got0[0]])))
    odd.append(swapped(even[1]))
    got1 = start_sums([1], together[0], [got0[0]])
    s0 = halves(together, [got0], [got1[0]])
    q0 = py(s0[0]), px(s0[1])
    s1 = halves(together, [got1], [s0[0]])
    q1 = py(s1[0]), px(s1[1])
    z2 = gate(z2, [s1[0]])
    z3 = over_col(z2, 2)
    even.append(halved(z2))
    odd.append(swapped(even[2]))
    d0, h0 = finish(together, [got0], *q0, (), [s1[0]])
    d01, h01 = finish(together, [got1], *q1, (("d", d0), ("h", h0)), [])
    first01 = gather_first(*d01)
    full01 = gather_second(*first01)
    even.append(halved(gate(z3, [first01[0], first01[1]])))
    odd.append(swapped(even[3]))
    got2 = [start_sums([2, 3], split[0], list(first01))]
    got2.append(start_sums([2, 3], split[1], [got2[0][0], full01[2], full01[3]]))
    ta, tb = gin(place_g, quarters(*full01), wg, wu, tok, [got2[1][0]])
    s2 = halves(split, got2, [tb])
    q2 = py(s2[0]), px(s2[1])
    d23, h_all = finish(split, got2, *q2, (("h", h01),), [])
    full23 = gather_second(*gather_first(*d23))
    h_full = quarters(*gather_second(*gather_first(*h_all)))
    full01, full23 = quarters(*full01), quarters(*full23)
    ta2, tb2 = gin(place_g, full23, wg, wu, tok, [])

    def both(a, b):
        return a.astype(F32) + over_col(b, 1).astype(F32)

    s01, s23 = both(ta, tb), both(ta2, tb2)
    r1 = over_col(s01[1].astype(BF), 2)
    r3 = over_col(s23[1].astype(BF), 2)
    r2 = over_col((s23[0] + r3.astype(F32)).astype(BF), 4)
    grad_in = (s01[0] + r1.astype(F32) + r2.astype(F32)).astype(BF)

    left = [full01[q] + full23[q] for q in range(4)]
    right = [e[0] for e in even[:2] + odd[:2] + even[2:] + odd[2:]]
    grad_gate, grad_up = wgrad(place_g, left, right, 2, width, [tb2])
    right = [e[1] for e in even + odd]
    (grad_down,) = wgrad(place_g, h_full, right, 1, width, [grad_up])
    return grad_in, grad_gate.T, grad_up.T, grad_down


def solution(mesh):
    placed = (P("col", "row"), P("col", "row"), P("row", "col"), P("row", "col"), P("col", "row"))
    fits = mesh.shape["row"] == 4 and mesh.shape["col"] == 8
    return jax.shard_map(
        grid_4_8 if fits else general,
        mesh=mesh,
        in_specs=placed,
        out_specs=(P("col", "row"), P("row", "col"), P("row", "col"), P("col", "row")),
        check_vma=False,
    )
```

```python
import functools

import jax
import jax.numpy as jnp
from jax import lax
from jax.experimental import pallas as pl
from jax.experimental.pallas import tpu as pltpu
from jax.sharding import PartitionSpec as P

BF = jnp.bfloat16
F32 = jnp.float32
VMEM_LIMIT = 56 * 1024 * 1024
TINY = pl.CostEstimate(flops=1, bytes_accessed=1, transcendentals=0)


def activations(gate, up, d_hidden):
    sig = 1.0 / (1.0 + jnp.exp(-gate))
    silu = gate * sig
    hidden = (silu * up).astype(BF)
    d_up = (d_hidden * silu).astype(BF)
    d_gate = (d_hidden * up * sig * (1.0 + gate * (1.0 - sig))).astype(BF)
    return hidden, d_gate, d_up


def general(inputs, upstream, w_gate, w_up, w_down):
    x_all = lax.all_gather(inputs, "col", axis=0, tiled=True)
    dy_all = lax.all_gather(upstream, "col", axis=0, tiled=True)
    back = (((1,), (1,)), ((), ()))
    terms = (
        jnp.dot(x_all, w_gate, preferred_element_type=F32),
        jnp.dot(x_all, w_up, preferred_element_type=F32),
        lax.dot_general(dy_all, w_down, back, preferred_element_type=F32),
    )
    sums = [
        lax.psum_scatter(t.astype(BF), "row", scatter_dimension=0, tiled=True).astype(F32)
        for t in terms
    ]
    hidden, d_gate, d_up = (
        lax.all_gather(a, "row", axis=0, tiled=True) for a in activations(*sums)
    )
    contract = (((0,), (0,)), ((), ()))
    grad_down = lax.dot_general(hidden, dy_all, contract, preferred_element_type=F32).astype(BF)
    grad_gate = lax.dot_general(x_all, d_gate, contract, preferred_element_type=F32).astype(BF)
    grad_up = lax.dot_general(x_all, d_up, contract, preferred_element_type=F32).astype(BF)
    term = lax.dot_general(d_gate, w_gate, back, preferred_element_type=F32)
    term = term + lax.dot_general(d_up, w_up, back, preferred_element_type=F32)
    grad_in = lax.psum_scatter(term.astype(BF), "col", scatter_dimension=0, tiled=True)
    return grad_in, grad_gate, grad_up, grad_down


def quarter_rows(width):
    return -(-width // 64) * 16


def masked(block, quarter, width):
    rows = block.shape[0]
    index = quarter * rows + lax.broadcasted_iota(jnp.int32, block.shape, 0)
    return jnp.where(index < width, block, jnp.zeros_like(block))


def order_only():
    return pl.BlockSpec(memory_space=pl.ANY)


def gate(a, after):
    return pl.pallas_call(
        lambda *refs: None,
        out_shape=jax.ShapeDtypeStruct(a.shape, a.dtype),
        in_specs=[order_only()] * (1 + len(after)),
        out_specs=order_only(),
        input_output_aliases={0: 0},
        cost_estimate=TINY,
    )(a, *after)


def entry_spec(a, index):
    if index is None:
        return pl.BlockSpec(a.shape, lambda s, p: (0,) * a.ndim)
    return pl.BlockSpec((None,) + a.shape[1:], lambda s, p: (index,) + (0,) * (a.ndim - 1))


SEND_FIRST = ((1, 0), (1, 1), (0, 0), (0, 1))
ORDER = ((0, 0), (0, 1), (1, 0), (1, 1))


def terms_kernel(width, n, lefts, place, *refs):
    kinds = sorted(set(lefts))
    blocks = refs[: n * len(kinds)]
    weights = refs[n * len(kinds) : n * len(kinds) + len(lefts)]
    send_a, keep_a, send_b, keep_b, both = refs[-5:]
    step = pl.program_id(0)
    tok = blocks[0].shape[0]

    @pl.when(step == 0)
    def _():
        for i, r in enumerate(blocks):
            both[i // n, (i % n) * tok : (i % n + 1) * tok, :] = r[...]

    dims = (((1,), (1,)), ((), ()))
    cut = n * tok // 2
    for i, w in enumerate(weights):
        left = both[kinds.index(lefts[i])]
        t = lax.dot_general(w[...], left, dims, preferred_element_type=F32)
        t = masked(t, place[step], width).astype(BF)
        for s, (dx, dy) in enumerate(SEND_FIRST):

            @pl.when(step == s)
            def _(t=t, i=i, dx=dx, dy=dy):
                (send_a if dx else keep_a)[dy, i] = t[:, :cut]
                (send_b if dy else keep_b)[dx, i] = t[:, cut:]


def terms(place, blocks, weights, lefts, after):
    n = len(blocks)
    used = [b[k] for k in sorted(set(lefts)) for b in blocks]
    width, feats = weights[0].shape
    rows = quarter_rows(width)
    tok = used[0][0].shape[-2]
    weight = pl.BlockSpec((rows, feats), lambda s, p: (p[s], 0))
    shape = (2, len(weights), rows, n * tok // 2)
    part = pl.BlockSpec(shape, lambda s, p: (0, 0, 0, 0))
    return pl.pallas_call(
        functools.partial(terms_kernel, width, n, lefts),
        out_shape=[jax.ShapeDtypeStruct(shape, BF)] * 4,
        grid_spec=pltpu.PrefetchScalarGridSpec(
            num_scalar_prefetch=1,
            grid=(4,),
            in_specs=[entry_spec(*e) for e in used]
            + [weight] * len(weights)
            + [order_only()] * len(after),
            out_specs=[part] * 4,
            scratch_shapes=[pltpu.VMEM((len(set(lefts)), n * tok, feats), BF)],
        ),
        compiler_params=pltpu.CompilerParams(vmem_limit_bytes=VMEM_LIMIT),
        cost_estimate=TINY,
    )(place, *[a for a, _ in used], *weights, *after)


def halves_kernel(groups, *refs):
    per = 2 * len(groups)
    for side in range(2):
        mine, out = refs[side * per : (side + 1) * per], refs[len(refs) - 2 + side]
        for g, group in enumerate(groups):
            for k, i in enumerate(group):
                total = mine[2 * g][0, k].astype(F32) + mine[2 * g + 1][0, k].astype(F32)
                out[i] = total.astype(BF)


def halves(groups, got, after):
    rows, tok = got[0][0].shape[2:]
    arrays = [v for ka, ra, _, _ in got for v in (ka, ra)]
    arrays += [v for _, _, kb, rb in got for v in (kb, rb)]
    specs = [pl.BlockSpec((1,) + a.shape[1:], lambda s: (1, 0, 0, 0)) for a in arrays]
    out = jax.ShapeDtypeStruct((3, rows, tok), BF)
    return pl.pallas_call(
        functools.partial(halves_kernel, groups),
        out_shape=[out, out],
        grid=(1,),
        in_specs=specs + [order_only()] * len(after),
        out_specs=[pl.BlockSpec(out.shape, lambda s: (0, 0, 0))] * 2,
        compiler_params=pltpu.CompilerParams(vmem_limit_bytes=VMEM_LIMIT),
        cost_estimate=TINY,
    )(*arrays, *after)


def act_kernel(groups, earlier, per, *refs):
    outs = refs[-4:]
    for side in range(2):
        mine = refs[side * per : (side + 1) * per]
        last = mine[2 * len(groups)]
        sums = [None] * 3
        for g, group in enumerate(groups):
            for k, i in enumerate(group):
                keep, got = mine[2 * g], mine[2 * g + 1]
                sums[i] = keep[0, k].astype(F32) + got[0, k].astype(F32) + last[i].astype(F32)
        hidden, d_gate, d_up = activations(*sums)
        d, h = outs[2 * side], outs[2 * side + 1]
        tok = hidden.shape[1]
        d[0, :, -tok:], d[1, :, -tok:], h[:, -tok:] = d_gate, d_up, hidden
        if "d" in earlier:
            d[:, :, :-tok] = mine[2 * len(groups) + 1][...]
        if "h" in earlier:
            h[:, :-tok] = mine[-1][...]


def act(groups, sides, earlier, after):
    rows, tok = sides[0][0].shape[2:]
    specs = []
    for a in sides[0]:
        block = (1,) + a.shape[1:] if a.ndim == 4 else a.shape
        specs.append(pl.BlockSpec(block, lambda s, n=a.ndim: (0,) * n))
    before = {k: sides[0][-len(earlier) + i].shape[-1] for i, k in enumerate(earlier)}
    d = jax.ShapeDtypeStruct((2, rows, before.get("d", 0) + tok), BF)
    h = jax.ShapeDtypeStruct((rows, before.get("h", 0) + tok), BF)
    dspec = pl.BlockSpec(d.shape, lambda s: (0, 0, 0))
    hspec = pl.BlockSpec(h.shape, lambda s: (0, 0))
    return pl.pallas_call(
        functools.partial(act_kernel, groups, earlier, len(specs)),
        out_shape=[d, h, d, h],
        grid=(1,),
        in_specs=specs * 2 + [order_only()] * len(after),
        out_specs=[dspec, hspec, dspec, hspec],
        compiler_params=pltpu.CompilerParams(vmem_limit_bytes=VMEM_LIMIT),
        cost_estimate=TINY,
    )(*sides[0], *sides[1], *after)


def gin_kernel(width, n, place, *refs):
    quarters, (wg, wu) = refs[: 4 * n], refs[4 * n : 4 * n + 2]
    ta, tb, total = refs[-3:]
    step = pl.program_id(0)
    dims = (((0,), (0,)), ((), ()))
    wgm = masked(wg[...], place[step], width)
    wum = masked(wu[...], place[step], width)
    for s in range(4):

        @pl.when(step == s)
        def _(s=s):
            mine = quarters[s * n : (s + 1) * n]
            dg = jnp.concatenate([r[0] for r in mine], axis=1)
            du = jnp.concatenate([r[1] for r in mine], axis=1)
            t = lax.dot_general(dg, wgm, dims, preferred_element_type=F32)
            t = t + lax.dot_general(du, wum, dims, preferred_element_type=F32)
            if s == 0:
                total[...] = t
            elif s < 3:
                total[...] += t
            else:
                t = t + total[...]
                blocks, tok, _ = ta.shape
                for j in range(blocks):
                    ta[j] = t[j * tok : (j + 1) * tok].astype(BF)
                    tb[j] = t[(blocks + j) * tok : (blocks + j + 1) * tok].astype(BF)


def gin(place, quarters, wg, wu, tok, after):
    n = len(quarters[0])
    width, feats = wg.shape
    rows = quarters[0][0][0].shape[-2]
    blocks = sum(a.shape[-1] for a, _ in quarters[0]) // (2 * tok)
    specs = [entry_spec(*e) for q in quarters for e in q]
    weight = pl.BlockSpec((rows, feats), lambda s, p: (p[s], 0))
    out = pl.BlockSpec((blocks, tok, feats), lambda s, p: (0, 0, 0))
    return pl.pallas_call(
        functools.partial(gin_kernel, width, n),
        out_shape=[jax.ShapeDtypeStruct((blocks, tok, feats), BF)] * 2,
        grid_spec=pltpu.PrefetchScalarGridSpec(
            num_scalar_prefetch=1,
            grid=(4,),
            in_specs=specs + [weight, weight] + [order_only()] * len(after),
            out_specs=[out, out],
            scratch_shapes=[pltpu.VMEM((2 * blocks * tok, feats), F32)],
        ),
        compiler_params=pltpu.CompilerParams(vmem_limit_bytes=VMEM_LIMIT),
        cost_estimate=TINY,
    )(place, *[a for q in quarters for a, _ in q], wg, wu, *after)


def wgrad_kernel(kinds, n, blocks, place, *refs):
    left, right = refs[: 4 * n], refs[4 * n : 4 * n + blocks]
    outs, toks = refs[-1 - kinds : -1], refs[-1]
    step = pl.program_id(0)
    tok = right[0].shape[0]

    @pl.when(step == 0)
    def _():
        for b in range(blocks):
            toks[b * tok : (b + 1) * tok, :] = right[b][...]

    for s in range(4):

        @pl.when(step == s)
        def _(s=s):
            mine = left[s * n : (s + 1) * n]
            for k in range(kinds):
                m = jnp.concatenate([r[k] if kinds > 1 else r[...] for r in mine], axis=1)
                outs[k][...] = jnp.dot(m, toks[...], preferred_element_type=F32).astype(BF)


def wgrad(place, left, right, kinds, width, after):
    n, blocks = len(left[0]), len(right)
    rows = left[0][0][0].shape[-2]
    tok, feats = right[0][0].shape[-2:]
    lspecs = [entry_spec(*e) for q in left for e in q]
    rspecs = [entry_spec(*e) for e in right]
    out = pl.BlockSpec((rows, feats), lambda s, p: (p[s], 0))
    return pl.pallas_call(
        functools.partial(wgrad_kernel, kinds, n, blocks),
        out_shape=[jax.ShapeDtypeStruct((width, feats), BF)] * kinds,
        grid_spec=pltpu.PrefetchScalarGridSpec(
            num_scalar_prefetch=1,
            grid=(4,),
            in_specs=lspecs + rspecs + [order_only()] * len(after),
            out_specs=[out] * kinds,
            scratch_shapes=[pltpu.VMEM((blocks * tok, feats), BF)],
        ),
        compiler_params=pltpu.CompilerParams(vmem_limit_bytes=VMEM_LIMIT),
        cost_estimate=TINY,
    )(place, *[a for q in left for a, _ in q], *[a for a, _ in right], *after)


def grid_4_8(inputs, upstream, w_gate, w_up, w_down):
    weights = (w_gate.T, w_up.T, w_down)
    wg, wu, _ = weights
    width = w_down.shape[0]
    tok = inputs.shape[0]
    row = lax.axis_index("row").astype(jnp.int32)
    x, y = row % 2, row // 2

    def place_of(pairs):
        return jnp.stack([2 * (x ^ dx) + (y ^ dy) for dx, dy in pairs])

    place_t, place_g = place_of(SEND_FIRST), place_of(ORDER)

    def over_row(a, bit):
        return lax.ppermute(a, "row", [(r, r ^ bit) for r in range(4)])

    def over_col(a, bits):
        return lax.ppermute(a, "col", [(c, c ^ bits) for c in range(8)])

    px, py = functools.partial(over_row, bit=1), functools.partial(over_row, bit=2)

    own = jnp.stack([inputs, upstream])
    def swapped(pair):
        return tuple((over_col(a if i is None else a[i], 1), None) for a, i in pair)

    def halved(a):
        return ((a, 0), (a, 1))

    even = [((inputs, None), (upstream, None))]
    odd = [swapped(even[0])]
    z1, z2 = over_col(own, 2), over_col(own, 4)

    split, together = ((0, 1), (2,)), ((0, 1, 2),)

    def start_sums(blocks, group, after):
        sa, ka, sb, kb = terms(
            place_t,
            [e[j] for e in (even, odd) for j in blocks],
            [weights[i] for i in group],
            [i // 2 for i in group],
            after,
        )
        return ka, px(sa), kb, py(sb)

    def finish(groups, got, qa, qb, before, after):
        sides = [
            [v for ka, ra, _, _ in got for v in (ka, ra)] + [qa],
            [v for _, _, kb, rb in got for v in (kb, rb)] + [qb],
        ]
        earlier = "".join(k for k, _ in before)
        for _, pair in before:
            for side, a in zip(sides, pair):
                side.append(a)
        da, ha, db, hb = act(groups, sides, earlier, after)
        return (da, db), (ha, hb)

    def gather_first(a, b):
        return jnp.stack([a, py(a)]), jnp.stack([b, px(b)])

    def gather_second(sa, sb):
        return sa, sb, px(sa), py(sb)

    def quarters(sa, sb, ra, rb):
        return (
            ((sa, 0), (sb, 0)),
            ((sa, 1), (rb, 0)),
            ((ra, 0), (sb, 1)),
            ((ra, 1), (rb, 1)),
        )

    got0 = start_sums([0], together[0], [])
    even.append(halved(gate(z1, [got0[0]])))
    odd.append(swapped(even[1]))
    got1 = start_sums([1], together[0], [got0[0]])
    s0 = halves(together, [got0], [got1[0]])
    q0 = py(s0[0]), px(s0[1])
    s1 = halves(together, [got1], [s0[0]])
    q1 = py(s1[0]), px(s1[1])
    z2 = gate(z2, [s1[0]])
    z3 = over_col(z2, 2)
    even.append(halved(z2))
    odd.append(swapped(even[2]))
    d0, h0 = finish(together, [got0], *q0, (), [s1[0]])
    d01, h01 = finish(together, [got1], *q1, (("d", d0), ("h", h0)), [])
    first01 = gather_first(*d01)
    full01 = gather_second(*first01)
    even.append(halved(gate(z3, [first01[0], first01[1]])))
    odd.append(swapped(even[3]))
    got2 = [start_sums([2, 3], split[0], list(first01))]
    got2.append(start_sums([2, 3], split[1], [got2[0][0], full01[2], full01[3]]))
    ta, tb = gin(place_g, quarters(*full01), wg, wu, tok, [got2[1][0]])
    s2 = halves(split, got2, [tb])
    q2 = py(s2[0]), px(s2[1])
    d23, h_all = finish(split, got2, *q2, (("h", h01),), [])
    full23 = gather_second(*gather_first(*d23))
    h_full = quarters(*gather_second(*gather_first(*h_all)))
    full01, full23 = quarters(*full01), quarters(*full23)
    ta2, tb2 = gin(place_g, full23, wg, wu, tok, [h_full[0][0][0], h_full[0][1][0]])

    def both(a, b):
        return a.astype(F32) + over_col(b, 1).astype(F32)

    s01, s23 = both(ta, tb), both(ta2, tb2)
    r1 = over_col(s01[1].astype(BF), 2)
    r3 = over_col(s23[1].astype(BF), 2)
    r2 = over_col((s23[0] + r3.astype(F32)).astype(BF), 4)
    grad_in = (s01[0] + r1.astype(F32) + r2.astype(F32)).astype(BF)

    left = [full01[q] + full23[q] for q in range(4)]
    right = [e[0] for e in even[:2] + odd[:2] + even[2:] + odd[2:]]
    grad_gate, grad_up = wgrad(place_g, left, right, 2, width, [tb2])
    right = [e[1] for e in even + odd]
    (grad_down,) = wgrad(place_g, h_full, right, 1, width, [grad_up])
    return grad_in, grad_gate.T, grad_up.T, grad_down


def solution(mesh):
    placed = (P("col", "row"), P("col", "row"), P("row", "col"), P("row", "col"), P("col", "row"))
    fits = mesh.shape["row"] == 4 and mesh.shape["col"] == 8
    return jax.shard_map(
        grid_4_8 if fits else general,
        mesh=mesh,
        in_specs=placed,
        out_specs=(P("col", "row"), P("row", "col"), P("row", "col"), P("col", "row")),
        check_vma=False,
    )
```

```python
import functools

import jax
import jax.numpy as jnp
from jax import lax
from jax.experimental import pallas as pl
from jax.experimental.pallas import tpu as pltpu
from jax.sharding import PartitionSpec as P

BF = jnp.bfloat16
F32 = jnp.float32
VMEM_LIMIT = 56 * 1024 * 1024
TINY = pl.CostEstimate(flops=1, bytes_accessed=1, transcendentals=0)


def activations(gate, up, d_hidden):
    sig = 1.0 / (1.0 + jnp.exp(-gate))
    silu = gate * sig
    hidden = (silu * up).astype(BF)
    d_up = (d_hidden * silu).astype(BF)
    d_gate = (d_hidden * up * sig * (1.0 + gate * (1.0 - sig))).astype(BF)
    return hidden, d_gate, d_up


def general(inputs, upstream, w_gate, w_up, w_down):
    x_all = lax.all_gather(inputs, "col", axis=0, tiled=True)
    dy_all = lax.all_gather(upstream, "col", axis=0, tiled=True)
    back = (((1,), (1,)), ((), ()))
    terms = (
        jnp.dot(x_all, w_gate, preferred_element_type=F32),
        jnp.dot(x_all, w_up, preferred_element_type=F32),
        lax.dot_general(dy_all, w_down, back, preferred_element_type=F32),
    )
    sums = [
        lax.psum_scatter(t.astype(BF), "row", scatter_dimension=0, tiled=True).astype(F32)
        for t in terms
    ]
    hidden, d_gate, d_up = (
        lax.all_gather(a, "row", axis=0, tiled=True) for a in activations(*sums)
    )
    contract = (((0,), (0,)), ((), ()))
    grad_down = lax.dot_general(hidden, dy_all, contract, preferred_element_type=F32).astype(BF)
    grad_gate = lax.dot_general(x_all, d_gate, contract, preferred_element_type=F32).astype(BF)
    grad_up = lax.dot_general(x_all, d_up, contract, preferred_element_type=F32).astype(BF)
    term = lax.dot_general(d_gate, w_gate, back, preferred_element_type=F32)
    term = term + lax.dot_general(d_up, w_up, back, preferred_element_type=F32)
    grad_in = lax.psum_scatter(term.astype(BF), "col", scatter_dimension=0, tiled=True)
    return grad_in, grad_gate, grad_up, grad_down


def quarter_rows(width):
    return -(-width // 64) * 16


def masked(block, quarter, width):
    rows = block.shape[0]
    index = quarter * rows + lax.broadcasted_iota(jnp.int32, block.shape, 0)
    return jnp.where(index < width, block, jnp.zeros_like(block))


def order_only():
    return pl.BlockSpec(memory_space=pl.ANY)


def gate(a, after):
    return pl.pallas_call(
        lambda *refs: None,
        out_shape=jax.ShapeDtypeStruct(a.shape, a.dtype),
        in_specs=[order_only()] * (1 + len(after)),
        out_specs=order_only(),
        input_output_aliases={0: 0},
        cost_estimate=TINY,
    )(a, *after)


def entry_spec(a, index):
    if index is None:
        return pl.BlockSpec(a.shape, lambda s, p: (0,) * a.ndim)
    return pl.BlockSpec((None,) + a.shape[1:], lambda s, p: (index,) + (0,) * (a.ndim - 1))


SEND_FIRST = ((1, 0), (1, 1), (0, 0), (0, 1))
ORDER = ((0, 0), (0, 1), (1, 0), (1, 1))


def terms_kernel(width, n, lefts, place, *refs):
    kinds = sorted(set(lefts))
    blocks = refs[: n * len(kinds)]
    weights = refs[n * len(kinds) : n * len(kinds) + len(lefts)]
    send_a, keep_a, send_b, keep_b, both = refs[-5:]
    step = pl.program_id(0)
    tok = blocks[0].shape[0]

    @pl.when(step == 0)
    def _():
        for i, r in enumerate(blocks):
            both[i // n, (i % n) * tok : (i % n + 1) * tok, :] = r[...]

    dims = (((1,), (1,)), ((), ()))
    cut = n * tok // 2
    for i, w in enumerate(weights):
        left = both[kinds.index(lefts[i])]
        t = lax.dot_general(w[...], left, dims, preferred_element_type=F32)
        t = masked(t, place[step], width).astype(BF)
        for s, (dx, dy) in enumerate(SEND_FIRST):

            @pl.when(step == s)
            def _(t=t, i=i, dx=dx, dy=dy):
                (send_a if dx else keep_a)[dy, i] = t[:, :cut]
                (send_b if dy else keep_b)[dx, i] = t[:, cut:]


def terms(place, blocks, weights, lefts, after):
    n = len(blocks)
    used = [b[k] for k in sorted(set(lefts)) for b in blocks]
    width, feats = weights[0].shape
    rows = quarter_rows(width)
    tok = used[0][0].shape[-2]
    weight = pl.BlockSpec((rows, feats), lambda s, p: (p[s], 0))
    shape = (2, len(weights), rows, n * tok // 2)
    part = pl.BlockSpec(shape, lambda s, p: (0, 0, 0, 0))
    return pl.pallas_call(
        functools.partial(terms_kernel, width, n, lefts),
        out_shape=[jax.ShapeDtypeStruct(shape, BF)] * 4,
        grid_spec=pltpu.PrefetchScalarGridSpec(
            num_scalar_prefetch=1,
            grid=(4,),
            in_specs=[entry_spec(*e) for e in used]
            + [weight] * len(weights)
            + [order_only()] * len(after),
            out_specs=[part] * 4,
            scratch_shapes=[pltpu.VMEM((len(set(lefts)), n * tok, feats), BF)],
        ),
        compiler_params=pltpu.CompilerParams(vmem_limit_bytes=VMEM_LIMIT),
        cost_estimate=TINY,
    )(place, *[a for a, _ in used], *weights, *after)


def halves_kernel(groups, *refs):
    per = 2 * len(groups)
    for side in range(2):
        mine, out = refs[side * per : (side + 1) * per], refs[len(refs) - 2 + side]
        for g, group in enumerate(groups):
            for k, i in enumerate(group):
                total = mine[2 * g][0, k].astype(F32) + mine[2 * g + 1][0, k].astype(F32)
                out[i] = total.astype(BF)


def halves(groups, got, after):
    rows, tok = got[0][0].shape[2:]
    arrays = [v for ka, ra, _, _ in got for v in (ka, ra)]
    arrays += [v for _, _, kb, rb in got for v in (kb, rb)]
    specs = [pl.BlockSpec((1,) + a.shape[1:], lambda s: (1, 0, 0, 0)) for a in arrays]
    out = jax.ShapeDtypeStruct((3, rows, tok), BF)
    return pl.pallas_call(
        functools.partial(halves_kernel, groups),
        out_shape=[out, out],
        grid=(1,),
        in_specs=specs + [order_only()] * len(after),
        out_specs=[pl.BlockSpec(out.shape, lambda s: (0, 0, 0))] * 2,
        compiler_params=pltpu.CompilerParams(vmem_limit_bytes=VMEM_LIMIT),
        cost_estimate=TINY,
    )(*arrays, *after)


def act_kernel(groups, earlier, per, *refs):
    outs = refs[-4:]
    for side in range(2):
        mine = refs[side * per : (side + 1) * per]
        last = mine[2 * len(groups)]
        sums = [None] * 3
        for g, group in enumerate(groups):
            for k, i in enumerate(group):
                keep, got = mine[2 * g], mine[2 * g + 1]
                sums[i] = keep[0, k].astype(F32) + got[0, k].astype(F32) + last[i].astype(F32)
        hidden, d_gate, d_up = activations(*sums)
        d, h = outs[2 * side], outs[2 * side + 1]
        tok = hidden.shape[1]
        d[0, :, -tok:], d[1, :, -tok:], h[:, -tok:] = d_gate, d_up, hidden
        if "d" in earlier:
            d[:, :, :-tok] = mine[2 * len(groups) + 1][...]
        if "h" in earlier:
            h[:, :-tok] = mine[-1][...]


def act(groups, sides, earlier, after):
    rows, tok = sides[0][0].shape[2:]
    specs = []
    for a in sides[0]:
        block = (1,) + a.shape[1:] if a.ndim == 4 else a.shape
        specs.append(pl.BlockSpec(block, lambda s, n=a.ndim: (0,) * n))
    before = {k: sides[0][-len(earlier) + i].shape[-1] for i, k in enumerate(earlier)}
    d = jax.ShapeDtypeStruct((2, rows, before.get("d", 0) + tok), BF)
    h = jax.ShapeDtypeStruct((rows, before.get("h", 0) + tok), BF)
    dspec = pl.BlockSpec(d.shape, lambda s: (0, 0, 0))
    hspec = pl.BlockSpec(h.shape, lambda s: (0, 0))
    return pl.pallas_call(
        functools.partial(act_kernel, groups, earlier, len(specs)),
        out_shape=[d, h, d, h],
        grid=(1,),
        in_specs=specs * 2 + [order_only()] * len(after),
        out_specs=[dspec, hspec, dspec, hspec],
        compiler_params=pltpu.CompilerParams(vmem_limit_bytes=VMEM_LIMIT),
        cost_estimate=TINY,
    )(*sides[0], *sides[1], *after)


def gin_kernel(width, n, place, *refs):
    quarters, (wg, wu) = refs[: 4 * n], refs[4 * n : 4 * n + 2]
    ta, tb, total = refs[-3:]
    step = pl.program_id(0)
    dims = (((0,), (0,)), ((), ()))
    wgm = masked(wg[...], place[step], width)
    wum = masked(wu[...], place[step], width)
    for s in range(4):

        @pl.when(step == s)
        def _(s=s):
            mine = quarters[s * n : (s + 1) * n]
            dg = jnp.concatenate([r[0] for r in mine], axis=1)
            du = jnp.concatenate([r[1] for r in mine], axis=1)
            t = lax.dot_general(dg, wgm, dims, preferred_element_type=F32)
            t = t + lax.dot_general(du, wum, dims, preferred_element_type=F32)
            if s == 0:
                total[...] = t
            elif s < 3:
                total[...] += t
            else:
                t = t + total[...]
                blocks, tok, _ = ta.shape
                for j in range(blocks):
                    ta[j] = t[j * tok : (j + 1) * tok].astype(BF)
                    tb[j] = t[(blocks + j) * tok : (blocks + j + 1) * tok].astype(BF)


def gin(place, quarters, wg, wu, tok, after):
    n = len(quarters[0])
    width, feats = wg.shape
    rows = quarters[0][0][0].shape[-2]
    blocks = sum(a.shape[-1] for a, _ in quarters[0]) // (2 * tok)
    specs = [entry_spec(*e) for q in quarters for e in q]
    weight = pl.BlockSpec((rows, feats), lambda s, p: (p[s], 0))
    out = pl.BlockSpec((blocks, tok, feats), lambda s, p: (0, 0, 0))
    return pl.pallas_call(
        functools.partial(gin_kernel, width, n),
        out_shape=[jax.ShapeDtypeStruct((blocks, tok, feats), BF)] * 2,
        grid_spec=pltpu.PrefetchScalarGridSpec(
            num_scalar_prefetch=1,
            grid=(4,),
            in_specs=specs + [weight, weight] + [order_only()] * len(after),
            out_specs=[out, out],
            scratch_shapes=[pltpu.VMEM((2 * blocks * tok, feats), F32)],
        ),
        compiler_params=pltpu.CompilerParams(vmem_limit_bytes=VMEM_LIMIT),
        cost_estimate=TINY,
    )(place, *[a for q in quarters for a, _ in q], wg, wu, *after)


def wgrad_kernel(kinds, n, blocks, place, *refs):
    left, right = refs[: 4 * n], refs[4 * n : 4 * n + blocks]
    outs, toks = refs[-1 - kinds : -1], refs[-1]
    step = pl.program_id(0)
    tok = right[0].shape[0]

    @pl.when(step == 0)
    def _():
        for b in range(blocks):
            toks[b * tok : (b + 1) * tok, :] = right[b][...]

    for s in range(4):

        @pl.when(step == s)
        def _(s=s):
            mine = left[s * n : (s + 1) * n]
            for k in range(kinds):
                m = jnp.concatenate([r[k] if kinds > 1 else r[...] for r in mine], axis=1)
                outs[k][...] = jnp.dot(m, toks[...], preferred_element_type=F32).astype(BF)


def wgrad(place, left, right, kinds, width, after):
    n, blocks = len(left[0]), len(right)
    rows = left[0][0][0].shape[-2]
    tok, feats = right[0][0].shape[-2:]
    lspecs = [entry_spec(*e) for q in left for e in q]
    rspecs = [entry_spec(*e) for e in right]
    out = pl.BlockSpec((rows, feats), lambda s, p: (p[s], 0))
    return pl.pallas_call(
        functools.partial(wgrad_kernel, kinds, n, blocks),
        out_shape=[jax.ShapeDtypeStruct((width, feats), BF)] * kinds,
        grid_spec=pltpu.PrefetchScalarGridSpec(
            num_scalar_prefetch=1,
            grid=(4,),
            in_specs=lspecs + rspecs + [order_only()] * len(after),
            out_specs=[out] * kinds,
            scratch_shapes=[pltpu.VMEM((blocks * tok, feats), BF)],
        ),
        compiler_params=pltpu.CompilerParams(vmem_limit_bytes=VMEM_LIMIT),
        cost_estimate=TINY,
    )(place, *[a for q in left for a, _ in q], *[a for a, _ in right], *after)


def grid_4_8(inputs, upstream, w_gate, w_up, w_down):
    weights = (w_gate.T, w_up.T, w_down)
    wg, wu, _ = weights
    width = w_down.shape[0]
    tok = inputs.shape[0]
    row = lax.axis_index("row").astype(jnp.int32)
    x, y = row % 2, row // 2

    def place_of(pairs):
        return jnp.stack([2 * (x ^ dx) + (y ^ dy) for dx, dy in pairs])

    place_t, place_g = place_of(SEND_FIRST), place_of(ORDER)

    def over_row(a, bit):
        return lax.ppermute(a, "row", [(r, r ^ bit) for r in range(4)])

    def over_col(a, bits):
        return lax.ppermute(a, "col", [(c, c ^ bits) for c in range(8)])

    px, py = functools.partial(over_row, bit=1), functools.partial(over_row, bit=2)

    own = jnp.stack([inputs, upstream])
    def swapped(pair):
        return tuple((over_col(a if i is None else a[i], 1), None) for a, i in pair)

    def halved(a):
        return ((a, 0), (a, 1))

    even = [((inputs, None), (upstream, None))]
    odd = [swapped(even[0])]
    z1, z2 = over_col(own, 2), over_col(own, 4)

    split, together = ((0, 1), (2,)), ((0, 1, 2),)

    def start_sums(blocks, group, after):
        sa, ka, sb, kb = terms(
            place_t,
            [e[j] for e in (even, odd) for j in blocks],
            [weights[i] for i in group],
            [i // 2 for i in group],
            after,
        )
        return ka, px(sa), kb, py(sb)

    def finish(groups, got, qa, qb, before, after):
        sides = [
            [v for ka, ra, _, _ in got for v in (ka, ra)] + [qa],
            [v for _, _, kb, rb in got for v in (kb, rb)] + [qb],
        ]
        earlier = "".join(k for k, _ in before)
        for _, pair in before:
            for side, a in zip(sides, pair):
                side.append(a)
        da, ha, db, hb = act(groups, sides, earlier, after)
        return (da, db), (ha, hb)

    def gather_first(a, b):
        return jnp.stack([a, py(a)]), jnp.stack([b, px(b)])

    def gather_second(sa, sb):
        return sa, sb, px(sa), py(sb)

    def quarters(sa, sb, ra, rb):
        return (
            ((sa, 0), (sb, 0)),
            ((sa, 1), (rb, 0)),
            ((ra, 0), (sb, 1)),
            ((ra, 1), (rb, 1)),
        )

    got0 = start_sums([0], together[0], [])
    even.append(halved(gate(z1, [got0[0]])))
    odd.append(swapped(even[1]))
    got1 = start_sums([1], together[0], [got0[0]])
    s0 = halves(together, [got0], [got1[0]])
    q0 = py(s0[0]), px(s0[1])
    s1 = halves(together, [got1], [s0[0]])
    q1 = py(s1[0]), px(s1[1])
    z2 = gate(z2, [s1[0]])
    z3 = over_col(z2, 2)
    even.append(halved(z2))
    odd.append(swapped(even[2]))
    d0, h0 = finish(together, [got0], *q0, (), [s1[0]])
    d01, h01 = finish(together, [got1], *q1, (("d", d0), ("h", h0)), [])
    first01 = gather_first(*d01)
    full01 = gather_second(*first01)
    even.append(halved(gate(z3, [first01[0], first01[1]])))
    odd.append(swapped(even[3]))
    got2 = [start_sums([2, 3], split[0], list(first01))]
    got2.append(start_sums([2, 3], split[1], [got2[0][0], full01[2], full01[3]]))
    ta, tb = gin(place_g, quarters(*full01), wg, wu, tok, [got2[1][0]])
    s2 = halves(split, got2, [tb])
    q2 = py(s2[0]), px(s2[1])
    d23, h_all = finish(split, got2, *q2, (("h", h01),), [])
    full23 = gather_second(*gather_first(*d23))
    h_full = quarters(*gather_second(*gather_first(*h_all)))
    full01, full23 = quarters(*full01), quarters(*full23)
    ta2, tb2 = gin(place_g, full23, wg, wu, tok, [])

    def both(a, b):
        return a.astype(F32) + over_col(b, 1).astype(F32)

    s01, s23 = both(ta, tb), both(ta2, tb2)
    r1 = over_col(s01[1].astype(BF), 2)
    r2 = over_col(s23[0].astype(BF), 4)
    r3 = over_col(s23[1].astype(BF), 6)
    grad_in = (s01[0] + r1.astype(F32) + r2.astype(F32) + r3.astype(F32)).astype(BF)

    left = [full01[q] + full23[q] for q in range(4)]
    right = [e[0] for e in even[:2] + odd[:2] + even[2:] + odd[2:]]
    grad_gate, grad_up = wgrad(place_g, left, right, 2, width, [tb2])
    right = [e[1] for e in even + odd]
    (grad_down,) = wgrad(place_g, h_full, right, 1, width, [grad_up])
    return grad_in, grad_gate.T, grad_up.T, grad_down


def solution(mesh):
    placed = (P("col", "row"), P("col", "row"), P("row", "col"), P("row", "col"), P("col", "row"))
    fits = mesh.shape["row"] == 4 and mesh.shape["col"] == 8
    return jax.shard_map(
        grid_4_8 if fits else general,
        mesh=mesh,
        in_specs=placed,
        out_specs=(P("col", "row"), P("row", "col"), P("row", "col"), P("col", "row")),
        check_vma=False,
    )
```
